256 devices in a mesh: tm: 4 (over y_lo, core), frame: 64 (over x, y_hi, z).
Axes of the slice: x: 4, y: 4 (y_hi: 2, y_lo: 2; y = y_hi * 2 + y_lo), z: 8, core: 2. Of those that a mesh axis runs over, the one named last changes fastest.
Arguments:
- queries: bfloat16 [1024, 128, 1280], P(('tm', 'frame')), may hold values from -10 to 10
- keys: bfloat16 [1024, 128, 1280], P(('tm', 'frame')), may hold values from -10 to 10
- values: bfloat16 [1024, 128, 1280], P(('tm', 'frame')), may hold values from -6 to 6
- key_frames: int32 [16], replicated, may hold values from 0 to 1023, as said below
Outputs:
- edited: bfloat16 [1024, 128, 1280], P(('tm', 'frame'))
The draws below stay inside these ranges and needn't reach their ends.
Inputs may be any that keep to these rules, and one draw needn't show every extreme that they name: `key_frames`: entries g * 4 to g * 4 + 3 are the keyframes of group g; the j-th of them lies among frames g * 256 + j * (64) to g * 256 + (j + 1) * 64 - 1. Frame 0 and frame 1024 - 1 are keyframes.
All inputs are finite; a program needn't handle non-finite values.
Results may differ from the reference program's by a relative error of at most 0.009.
Values may be sent and summed in bfloat16 or wider, within the bound.
No kernel may reach another device: no remote copies, remote signals or barrier semaphores. Data moves between devices by JAX's collectives and lax.ppermute only.
A program may use at most 128 MiB of HBM per device.

```python
import jax
import jax.numpy as jnp
from jax import lax

HEADS = 20
HEAD_DIM = 64
D = 1280
TOK = 128
KPG = 4
GROUP_FRAMES = 256
FRAMES = 1024
KEYS = 16


def keyframe_positions(key):
    stream = jax.random.fold_in(key, 101)
    group_count = KEYS // KPG
    stratum = GROUP_FRAMES // KPG
    offsets = jax.random.randint(stream, (group_count, KPG), 0, stratum, dtype=jnp.int32)
    starts = jnp.arange(group_count, dtype=jnp.int32)[:, None] * GROUP_FRAMES + jnp.arange(KPG, dtype=jnp.int32)[None, :] * stratum
    chosen = starts + offsets
    chosen = chosen.at[0, 0].set(0)
    chosen = chosen.at[group_count - 1, KPG - 1].set(FRAMES - 1)
    return chosen.reshape(-1).astype(jnp.int32)


def draw_key_frames(key, part):
    return keyframe_positions(key)


def draw_keys(key, part):
    stream = jax.random.fold_in(key, 2)
    field = jnp.clip(jax.random.normal(stream, (FRAMES, TOK, D), jnp.float32), -6.0, 6.0)
    return field.astype(jnp.bfloat16)


def draw_queries(key, part):
    stream = jax.random.fold_in(key, 3)
    field = jnp.clip(jax.random.normal(stream, (FRAMES, TOK, D), jnp.float32), -6.0, 6.0)
    return field.astype(jnp.bfloat16)


def level_of(own_key, shape, cuts, least, top_value):
    factor_of, own = 1.0, jax.random.fold_in(own_key, 6)
    for dim, shards_of in cuts:
        steps = jnp.exp(jax.random.uniform(jax.random.fold_in(own, dim), (shards_of,), jnp.float32, least / len(cuts), top_value / len(cuts)))
        factor_of = factor_of * jnp.repeat(steps, shape[dim] // shards_of).reshape([-1 if axis == dim else 1 for axis in range(len(shape))])
    return factor_of


def normal_values(stream_key, dims, width, bound, shards=(), kind=jnp.bfloat16):
    values = jax.random.normal(stream_key, dims, jnp.float32) * width
    if len(shards) > 0:
        values = level_of(stream_key, dims, shards, -0.22, 0.18) * values
    return jnp.clip(values, min=-bound, max=bound).astype(kind)


def setup_inputs(seed: int = 0) -> dict:
    arg_keys = jax.random.split(jax.random.key(seed), 5)
    return {
        "queries": draw_queries(jax.random.fold_in(arg_keys[4], 71), 0),
        "keys": draw_keys(jax.random.fold_in(arg_keys[4], 71), 0),
        "values": normal_values(arg_keys[2], (FRAMES, TOK, D), 1.0, 6.0, ((0, 256),)),
        "key_frames": draw_key_frames(jax.random.fold_in(arg_keys[4], 71), 0),
    }


def attend(query_rows, key_rows, value_rows):
    row_count = query_rows.shape[0]
    query_heads = query_rows.reshape(row_count, HEADS, HEAD_DIM).astype(jnp.float32)
    key_heads = key_rows.reshape(-1, HEADS, HEAD_DIM).astype(jnp.float32)
    value_heads = value_rows.reshape(-1, HEADS, HEAD_DIM).astype(jnp.float32)
    scores = jnp.einsum("rhd,khd->hrk", query_heads, key_heads) * (HEAD_DIM ** -0.5)
    highest = jnp.max(scores, axis=2, keepdims=True)
    exponent = jnp.exp(scores - highest)
    row_total = jnp.sum(exponent, axis=2)
    weights = lax.optimization_barrier(exponent.astype(jnp.bfloat16))
    blended = jnp.einsum("hrk,khd->rhd", weights.astype(jnp.float32), value_heads)
    blended = blended / jnp.transpose(row_total)[:, :, None]
    return blended.reshape(row_count, HEADS * HEAD_DIM).astype(jnp.bfloat16)


def reference(queries, keys, values, key_frames):
    keyframe_keys = keys[key_frames]
    keyframe_values = values[key_frames]

    def one_frame(frame_number):
        group_index = frame_number // GROUP_FRAMES
        own_query = lax.dynamic_index_in_dim(queries, frame_number, 0, keepdims=False)
        own_keys = lax.dynamic_index_in_dim(keys, frame_number, 0, keepdims=False)
        own_values = lax.dynamic_index_in_dim(values, frame_number, 0, keepdims=False)
        start = (group_index * KPG).astype(jnp.int32)
        group_keys = lax.dynamic_slice_in_dim(keyframe_keys, start, KPG, 0).reshape(KPG * TOK, -1)
        group_values = lax.dynamic_slice_in_dim(keyframe_values, start, KPG, 0).reshape(KPG * TOK, -1)
        context_keys = jnp.concatenate([own_keys, group_keys], axis=0)
        context_values = jnp.concatenate([own_values, group_values], axis=0)
        return attend(own_query, context_keys, context_values)

    plain_out = lax.map(one_frame, jnp.arange(FRAMES, dtype=jnp.int32))
    all_keys = keyframe_keys.reshape(KEYS * TOK, -1)
    all_values = keyframe_values.reshape(KEYS * TOK, -1)

    def one_keyframe(frame_number):
        own_query = lax.dynamic_index_in_dim(queries, frame_number, 0, keepdims=False)
        return attend(own_query, all_keys, all_values)

    joint_out = lax.map(one_keyframe, key_frames)
    return plain_out.at[key_frames].set(joint_out)
```

```python
import jax
import jax.numpy as jnp
from jax import lax
from jax.experimental import pallas as pl
from jax.experimental.pallas import tpu as pltpu
from jax.sharding import PartitionSpec as P

HEADS = 20
HEAD_DIM = 64
KPG = 4
WIDE = 2 * HEAD_DIM
PAIRS = HEADS // 2
PLANES, ROWS_Y, RING = 4, 2, 8
QUARTERS = 4
VMEM_BYTES = 32 * 1024 * 1024
PLAIN_VMEM_BYTES = 60 * 1024 * 1024


def hop(x=0, y=0, z=0):
    pairs = []
    for member in range(PLANES * ROWS_Y * RING):
        px, py, pz = member // (ROWS_Y * RING), (member // RING) % ROWS_Y, member % RING
        target = ((px + x) % PLANES) * ROWS_Y * RING + ((py + y) % ROWS_Y) * RING + (pz + z) % RING
        pairs.append((member, target))
    return pairs


def send(array, **steps):
    return lax.ppermute(array, "frame", hop(**steps))


def swap_groups(array, mask):
    return lax.ppermute(array, "tm", [(group, group ^ mask) for group in range(4)])


def dot_last(a, b):
    return lax.dot_general(a, b, (((1,), (1,)), ((), ())), preferred_element_type=jnp.float32)


def dot_first(a, b):
    return lax.dot_general(a, b, (((0,), (0,)), ((), ())), preferred_element_type=jnp.float32)


def keep_one_head(array, other):
    low = lax.broadcasted_iota(jnp.int32, (1, WIDE), 1) < HEAD_DIM
    other = jnp.full((), other, array.dtype)
    return jnp.where(low, array, other), jnp.where(low, other, array)


def attend_pair(query, keys, values):
    sums, tops = [], []
    query = query * jnp.bfloat16(HEAD_DIM ** -0.5)
    for masked, extended in zip(keep_one_head(query, 0), keep_one_head(values, 1)):
        scores = dot_last(keys, masked)
        tops.append(jnp.max(scores, axis=0, keepdims=True))
        weights = jnp.exp(scores - tops[-1]).astype(jnp.bfloat16)
        sums.append(dot_first(extended, weights))
    totals = [sums[0][HEAD_DIM:HEAD_DIM + 1], sums[1][:1]]
    blended = jnp.concatenate([sums[0][:HEAD_DIM] / totals[0], sums[1][HEAD_DIM:] / totals[1]], axis=0)
    return blended.T, tops, totals


def columns_of(pair):
    return slice(pair * WIDE, (pair + 1) * WIDE)


def gathered(refs, which, columns):
    return [ref[:, which, :, columns].reshape(-1, WIDE) for ref in refs]


def whole(array):
    return pl.BlockSpec(array.shape, lambda i, *_: (0,) * array.ndim)


def plain_kernel(q_ref, k_ref, v_ref, *rest):
    group_refs, o_ref = rest[:-1], rest[-1]
    for pair in range(PAIRS):
        columns = columns_of(pair)
        keys = jnp.concatenate(gathered(group_refs, 0, columns) + [k_ref[0, :, columns]], axis=0)
        values = jnp.concatenate(gathered(group_refs, 1, columns) + [v_ref[0, :, columns]], axis=0)
        blended, _, _ = attend_pair(q_ref[0, :, columns], keys, values)
        o_ref[0, :, columns] = blended.astype(o_ref.dtype)


def plain_attend(queries, keys, values, blocks):
    frames, tokens, width = queries.shape
    own = pl.BlockSpec((1, tokens, width), lambda i: (i, 0, 0))
    return pl.pallas_call(
        plain_kernel,
        grid=(frames,),
        in_specs=[own, own, own] + [whole(b) for b in blocks],
        out_specs=own,
        out_shape=jax.ShapeDtypeStruct(queries.shape, queries.dtype),
        compiler_params=pltpu.CompilerParams(vmem_limit_bytes=PLAIN_VMEM_BYTES),
        cost_estimate=pl.CostEstimate(
            flops=4 * frames * tokens * 640 * width,
            bytes_accessed=8 * frames * tokens * width + 4 * 512 * width,
            transcendentals=frames * tokens * 640 * HEADS,
        ),
        name="plain_attend",
    )(queries, keys, values, *blocks)


def level_columns(levels):
    high = levels.astype(jnp.bfloat16).astype(jnp.float32)
    middle = (levels - high).astype(jnp.bfloat16).astype(jnp.float32)
    low = levels - high - middle
    return jnp.concatenate([high, middle, low, jnp.zeros_like(low)], axis=0).T.astype(jnp.bfloat16)


def levels_of(columns):
    parts = columns.astype(jnp.float32)
    return parts + pltpu.roll(parts, WIDE - 32, 1) + pltpu.roll(parts, WIDE - 64, 1)


def joint_kernel(facts_ref, side_ref, core_ref, *rest):
    group_refs, kept_ref, sent_ref, level_ref = rest[:-3], rest[-3], rest[-2], rest[-1]
    slot = pl.program_id(0)

    def attend(q_ref, o_ref):
        level_ref[...] = jnp.zeros_like(level_ref)
        for pair in range(PAIRS):
            columns = columns_of(pair)
            keys = jnp.concatenate(gathered(group_refs, 0, columns), axis=0)
            values = jnp.concatenate(gathered(group_refs, 1, columns), axis=0)
            blended, tops, totals = attend_pair(q_ref[0, :, columns], keys, values)
            o_ref[0, :, columns] = blended.astype(o_ref.dtype)
            for head in range(2):
                level_ref[2 * pair + head:2 * pair + head + 1] = tops[head] + jnp.log(totals[head])
        o_ref[0, :, HEADS * HEAD_DIM:] = level_columns(level_ref[...])

    wanted = facts_ref[slot] != 0
    pl.when(wanted & (slot < 2))(lambda: attend(core_ref, sent_ref))
    pl.when(wanted & (slot >= 2))(lambda: attend(side_ref, kept_ref))


def joint_attend(facts, side, core, blocks):
    _, tokens, width = side.shape
    first = lambda columns: pl.BlockSpec((1, tokens, columns), lambda i, f: (jnp.minimum(i, 1), 0, 0))
    last = lambda columns: pl.BlockSpec((1, tokens, columns), lambda i, f: (jnp.maximum(i - 2, 0), 0, 0))
    part = jax.ShapeDtypeStruct((2, tokens, width + WIDE), jnp.bfloat16)
    return pl.pallas_call(
        joint_kernel,
        grid_spec=pltpu.PrefetchScalarGridSpec(
            num_scalar_prefetch=1,
            grid=(4,),
            in_specs=[last(width), first(width)] + [whole(b) for b in blocks],
            out_specs=[last(width + WIDE), first(width + WIDE)],
            scratch_shapes=[pltpu.VMEM((32, tokens), jnp.float32)],
        ),
        out_shape=[part, part],
        compiler_params=pltpu.CompilerParams(vmem_limit_bytes=VMEM_BYTES),
        cost_estimate=pl.CostEstimate(
            flops=4 * tokens * 512 * width, bytes_accessed=4 * 512 * width, transcendentals=tokens * 512 * HEADS
        ),
        name="joint_attend",
    )(facts, side, core, *blocks)


def merged(a, b):
    width = HEADS * HEAD_DIM
    low = lax.broadcasted_iota(jnp.int32, (1, WIDE), 1) < HEAD_DIM
    level_a, level_b = levels_of(a[:, width:]), levels_of(b[:, width:])
    top = jnp.maximum(level_a, level_b)
    weight_a, weight_b = jnp.exp(level_a - top), jnp.exp(level_b - top)
    total = weight_a + weight_b
    weight_a, weight_b = weight_a / total, weight_b / total
    blended = []
    for pair in range(PAIRS):
        columns = columns_of(pair)
        first, second = slice(2 * pair, 2 * pair + 1), slice(2 * pair + 1, 2 * pair + 2)
        ratio_a = jnp.where(low, weight_a[:, first], weight_a[:, second])
        ratio_b = jnp.where(low, weight_b[:, first], weight_b[:, second])
        blended.append(a[:, columns].astype(jnp.float32) * ratio_a + b[:, columns].astype(jnp.float32) * ratio_b)
    return blended, top + jnp.log(total)


def merge_kernel(facts_ref, a_ref, b_ref, kept_ref, sent_ref):
    for slot, o_ref in enumerate((kept_ref, sent_ref)):

        @pl.when(facts_ref[2 + slot] != 0)
        def _():
            blended, level = merged(a_ref[slot], b_ref[slot])
            for pair in range(PAIRS):
                o_ref[:, columns_of(pair)] = blended[pair].astype(o_ref.dtype)
            o_ref[:, HEADS * HEAD_DIM:] = level_columns(level.T[:32])


def merge(facts, a, b):
    _, tokens, width = b.shape
    part = jax.ShapeDtypeStruct((tokens, width), b.dtype)
    return pl.pallas_call(
        merge_kernel,
        grid_spec=pltpu.PrefetchScalarGridSpec(
            num_scalar_prefetch=1, grid=(1,), in_specs=[whole(a), whole(b)], out_specs=[whole(part), whole(part)]
        ),
        out_shape=[part, part],
        compiler_params=pltpu.CompilerParams(vmem_limit_bytes=VMEM_BYTES),
        name="merge_partials",
    )(facts, a, b)


def place_kernel(facts_ref, a_ref, b_ref, plain_ref, o_ref):
    o_ref[...] = plain_ref[...]

    @pl.when(facts_ref[2] != 0)
    def _():
        blended, _ = merged(a_ref[...], b_ref[...])
        for pair in range(PAIRS):
            o_ref[0, :, columns_of(pair)] = blended[pair].astype(o_ref.dtype)


def place(facts, a, b, plain):
    tokens, width = plain.shape[1:]
    there = pl.BlockSpec((1, tokens, width), lambda i, f: (f[4], 0, 0))
    return pl.pallas_call(
        place_kernel,
        grid_spec=pltpu.PrefetchScalarGridSpec(
            num_scalar_prefetch=1, grid=(1,), in_specs=[whole(a), whole(b), there], out_specs=there
        ),
        out_shape=jax.ShapeDtypeStruct(plain.shape, plain.dtype),
        input_output_aliases={3: 0},
        compiler_params=pltpu.CompilerParams(vmem_limit_bytes=VMEM_BYTES),
        name="place_joint",
    )(facts, a, b, plain)


def body(queries, keys, values, key_frames):
    frames_here, tokens, width = queries.shape
    group = lax.axis_index("tm")
    member = lax.axis_index("frame")
    x, y, z = member // (ROWS_Y * RING), (member // RING) % ROWS_Y, member % RING
    group_frames = frames_here * lax.axis_size("frame")
    listed = jnp.arange(key_frames.shape[0], dtype=jnp.int32)
    pick = lambda entry: jnp.sum(jnp.where(listed == entry, key_frames, 0))
    local = pick(group * KPG + x) - group * group_frames
    owner, slot = local // frames_here, local % frames_here
    owner_y, owner_z = (owner // RING) % ROWS_Y, owner % RING
    away = (z - owner_z) % RING

    share = tokens // QUARTERS

    def quarter(index):
        start = (index % QUARTERS) * share
        return jnp.concatenate(
            [lax.dynamic_slice(a, (slot, start, 0), (1, share, width)) for a in (keys, values)]
        )

    mine = quarter(z)
    right, left, second = send(quarter(z + 1), z=1), send(quarter(z - 1), z=-1), send(quarter(z + 2), z=2)
    mine = jnp.where(away == 1, right, jnp.where(away == RING - 1, left, jnp.where(away == 2, second, mine)))
    filled = (away <= 2) | (away == RING - 1)
    mine = jnp.where(filled, mine, send(mine, z=RING // 2))
    mine = jnp.where(y == owner_y, mine, send(mine, y=1))
    second, right, left = send(mine, z=2), send(mine, z=1), send(mine, z=-1)
    half_a, half_b = jnp.stack([mine, right]), jnp.stack([left, second])
    right_a, left_b = send(half_a, x=1), send(half_b, x=-1)
    right_b, left_a = send(half_b, x=1), send(half_a, x=-1)
    own_query = lax.dynamic_index_in_dim(queries, slot, 0, keepdims=True)
    order = jnp.stack([group ^ 1, group ^ 3, group, group ^ 2])
    frames_of = jnp.sum(jnp.where(listed == order[:, None] * KPG + x, key_frames, 0), axis=1)
    wanted = (frames_of // frames_here == order * lax.axis_size("frame") + member).astype(jnp.int32)
    facts = jnp.concatenate([wanted, slot[None]])
    own_query, facts, half_b = lax.optimization_barrier((own_query, facts, half_b))
    side_query = jnp.concatenate([own_query, swap_groups(own_query, 2)])
    core_query = swap_groups(side_query, 1)
    far_a, far_b = send(right_a, x=1), send(left_b, x=-1)
    blocks = (half_a, half_b, right_a, right_b, left_a, left_b, far_a, far_b)

    kept, sent = joint_attend(facts, side_query, core_query, blocks)
    there = swap_groups(sent, 1)
    kept, sent = merge(facts, kept, there)
    there = swap_groups(sent, 2)
    plain = plain_attend(queries, keys, values, blocks)
    return place(facts, kept, there, plain)


def solution(mesh):
    placed = P(("tm", "frame"), None, None)
    return jax.shard_map(
        body, mesh=mesh, in_specs=(placed, placed, placed, P()), out_specs=placed, check_vma=False
    )
```

```python
import jax
import jax.numpy as jnp
from jax import lax
from jax.experimental import pallas as pl
from jax.experimental.pallas import tpu as pltpu
from jax.sharding import PartitionSpec as P

HEADS = 20
HEAD_DIM = 64
KPG = 4
WIDE = 2 * HEAD_DIM
PAIRS = HEADS // 2
PLANES, ROWS_Y, RING = 4, 2, 8
QUARTERS = 4
VMEM_BYTES = 32 * 1024 * 1024
PLAIN_VMEM_BYTES = 60 * 1024 * 1024


def hop(x=0, y=0, z=0):
    pairs = []
    for member in range(PLANES * ROWS_Y * RING):
        px, py, pz = member // (ROWS_Y * RING), (member // RING) % ROWS_Y, member % RING
        target = ((px + x) % PLANES) * ROWS_Y * RING + ((py + y) % ROWS_Y) * RING + (pz + z) % RING
        pairs.append((member, target))
    return pairs


def send(array, **steps):
    return lax.ppermute(array, "frame", hop(**steps))


def swap_groups(array, mask):
    return lax.ppermute(array, "tm", [(group, group ^ mask) for group in range(4)])


def dot_last(a, b):
    return lax.dot_general(a, b, (((1,), (1,)), ((), ())), preferred_element_type=jnp.float32)


def dot_first(a, b):
    return lax.dot_general(a, b, (((0,), (0,)), ((), ())), preferred_element_type=jnp.float32)


def keep_one_head(array, other):
    low = lax.broadcasted_iota(jnp.int32, (1, WIDE), 1) < HEAD_DIM
    other = jnp.full((), other, array.dtype)
    return jnp.where(low, array, other), jnp.where(low, other, array)


def attend_pair(query, keys, values):
    sums, tops = [], []
    query = query * jnp.bfloat16(HEAD_DIM ** -0.5)
    for masked, extended in zip(keep_one_head(query, 0), keep_one_head(values, 1)):
        scores = dot_last(keys, masked)
        tops.append(jnp.max(scores, axis=0, keepdims=True))
        weights = jnp.exp(scores - tops[-1]).astype(jnp.bfloat16)
        sums.append(dot_first(extended, weights))
    totals = [sums[0][HEAD_DIM:HEAD_DIM + 1], sums[1][:1]]
    blended = jnp.concatenate([sums[0][:HEAD_DIM] / totals[0], sums[1][HEAD_DIM:] / totals[1]], axis=0)
    return blended.T, tops, totals


def columns_of(pair):
    return slice(pair * WIDE, (pair + 1) * WIDE)


def gathered(refs, which, columns):
    return [ref[:, which, :, columns].reshape(-1, WIDE) for ref in refs]


def whole(array):
    return pl.BlockSpec(array.shape, lambda i, *_: (0,) * array.ndim)


def plain_kernel(facts_ref, q_ref, k_ref, v_ref, *rest):
    group_refs, o_ref = rest[:-1], rest[-1]

    @pl.when((facts_ref[2] == 0) | (facts_ref[4] != pl.program_id(0)))
    def _():
        for pair in range(PAIRS):
            columns = columns_of(pair)
            keys = jnp.concatenate(gathered(group_refs, 0, columns) + [k_ref[0, :, columns]], axis=0)
            values = jnp.concatenate(gathered(group_refs, 1, columns) + [v_ref[0, :, columns]], axis=0)
            blended, _, _ = attend_pair(q_ref[0, :, columns], keys, values)
            o_ref[0, :, columns] = blended.astype(o_ref.dtype)


def plain_attend(facts, queries, keys, values, blocks):
    frames, tokens, width = queries.shape
    own = pl.BlockSpec((1, tokens, width), lambda i, f: (i, 0, 0))
    return pl.pallas_call(
        plain_kernel,
        grid_spec=pltpu.PrefetchScalarGridSpec(
            num_scalar_prefetch=1,
            grid=(frames,),
            in_specs=[own, own, own] + [whole(b) for b in blocks],
            out_specs=own,
        ),
        out_shape=jax.ShapeDtypeStruct(queries.shape, queries.dtype),
        compiler_params=pltpu.CompilerParams(vmem_limit_bytes=PLAIN_VMEM_BYTES),
        cost_estimate=pl.CostEstimate(
            flops=4 * frames * tokens * 640 * width,
            bytes_accessed=8 * frames * tokens * width + 4 * 512 * width,
            transcendentals=frames * tokens * 640 * HEADS,
        ),
        name="plain_attend",
    )(facts, queries, keys, values, *blocks)


def level_columns(levels):
    high = levels.astype(jnp.bfloat16).astype(jnp.float32)
    middle = (levels - high).astype(jnp.bfloat16).astype(jnp.float32)
    low = levels - high - middle
    return jnp.concatenate([high, middle, low, jnp.zeros_like(low)], axis=0).T.astype(jnp.bfloat16)


def levels_of(columns):
    parts = columns.astype(jnp.float32)
    return parts + pltpu.roll(parts, WIDE - 32, 1) + pltpu.roll(parts, WIDE - 64, 1)


def joint_kernel(facts_ref, side_ref, core_ref, *rest):
    group_refs, kept_ref, sent_ref, level_ref = rest[:-3], rest[-3], rest[-2], rest[-1]

    def attend(slot, q_ref, o_ref):
        level_ref[...] = jnp.zeros_like(level_ref)
        for pair in range(PAIRS):
            columns = columns_of(pair)
            keys = jnp.concatenate(gathered(group_refs, 0, columns), axis=0)
            values = jnp.concatenate(gathered(group_refs, 1, columns), axis=0)
            blended, tops, totals = attend_pair(q_ref[slot, :, columns], keys, values)
            o_ref[slot, :, columns] = blended.astype(o_ref.dtype)
            for head in range(2):
                level_ref[2 * pair + head:2 * pair + head + 1] = tops[head] + jnp.log(totals[head])
        o_ref[slot, :, HEADS * HEAD_DIM:] = level_columns(level_ref[...])

    for slot in range(2):
        pl.when(facts_ref[slot] != 0)(lambda: attend(slot, core_ref, sent_ref))
        pl.when(facts_ref[2 + slot] != 0)(lambda: attend(slot, side_ref, kept_ref))


SCALARS = pl.BlockSpec(memory_space=pltpu.SMEM)
VECTORS = pl.BlockSpec(memory_space=pltpu.VMEM)


def joint_attend(facts, side, core, blocks):
    frames, tokens, width = side.shape
    part = jax.ShapeDtypeStruct((frames, tokens, width + WIDE), jnp.bfloat16)
    return pl.pallas_call(
        joint_kernel,
        in_specs=[SCALARS] + [VECTORS] * (2 + len(blocks)),
        out_specs=[VECTORS, VECTORS],
        scratch_shapes=[pltpu.VMEM((32, tokens), jnp.float32)],
        out_shape=[part, part],
        compiler_params=pltpu.CompilerParams(vmem_limit_bytes=VMEM_BYTES),
        cost_estimate=pl.CostEstimate(
            flops=4 * tokens * 512 * width, bytes_accessed=4 * 512 * width, transcendentals=tokens * 512 * HEADS
        ),
        name="joint_attend",
    )(facts, side, core, *blocks)


def merged(a, b):
    width = HEADS * HEAD_DIM
    low = lax.broadcasted_iota(jnp.int32, (1, WIDE), 1) < HEAD_DIM
    level_a, level_b = levels_of(a[:, width:]), levels_of(b[:, width:])
    top = jnp.maximum(level_a, level_b)
    weight_a, weight_b = jnp.exp(level_a - top), jnp.exp(level_b - top)
    total = weight_a + weight_b
    weight_a, weight_b = weight_a / total, weight_b / total
    blended = []
    for pair in range(PAIRS):
        columns = columns_of(pair)
        first, second = slice(2 * pair, 2 * pair + 1), slice(2 * pair + 1, 2 * pair + 2)
        ratio_a = jnp.where(low, weight_a[:, first], weight_a[:, second])
        ratio_b = jnp.where(low, weight_b[:, first], weight_b[:, second])
        blended.append(a[:, columns].astype(jnp.float32) * ratio_a + b[:, columns].astype(jnp.float32) * ratio_b)
    return blended, top + jnp.log(total)


def merge_kernel(facts_ref, a_ref, b_ref, kept_ref, sent_ref):
    for slot, o_ref in enumerate((kept_ref, sent_ref)):

        @pl.when(facts_ref[2 + slot] != 0)
        def _():
            blended, level = merged(a_ref[slot], b_ref[slot])
            for pair in range(PAIRS):
                o_ref[:, columns_of(pair)] = blended[pair].astype(o_ref.dtype)
            o_ref[:, HEADS * HEAD_DIM:] = level_columns(level.T[:32])


def merge(facts, a, b):
    _, tokens, width = b.shape
    part = jax.ShapeDtypeStruct((tokens, width), b.dtype)
    return pl.pallas_call(
        merge_kernel,
        in_specs=[SCALARS, VECTORS, VECTORS],
        out_specs=[VECTORS, VECTORS],
        out_shape=[part, part],
        compiler_params=pltpu.CompilerParams(vmem_limit_bytes=VMEM_BYTES),
        name="merge_partials",
    )(facts, a, b)


def place_kernel(facts_ref, a_ref, b_ref, plain_ref, o_ref, rows_ref, done):
    @pl.when(facts_ref[2] != 0)
    def _():
        blended, _ = merged(a_ref[...], b_ref[...])
        for pair in range(PAIRS):
            rows_ref[0, :, columns_of(pair)] = blended[pair].astype(rows_ref.dtype)
        copy = pltpu.make_async_copy(rows_ref, o_ref.at[pl.ds(facts_ref[4], 1)], done)
        copy.start()
        copy.wait()


def place(facts, a, b, plain):
    return pl.pallas_call(
        place_kernel,
        in_specs=[SCALARS, VECTORS, VECTORS, pl.BlockSpec(memory_space=pl.ANY)],
        out_specs=pl.BlockSpec(memory_space=pl.ANY),
        scratch_shapes=[pltpu.VMEM((1, *plain.shape[1:]), plain.dtype), pltpu.SemaphoreType.DMA],
        out_shape=jax.ShapeDtypeStruct(plain.shape, plain.dtype),
        input_output_aliases={3: 0},
        compiler_params=pltpu.CompilerParams(vmem_limit_bytes=VMEM_BYTES),
        name="place_joint",
    )(facts, a, b, plain)


def body(queries, keys, values, key_frames):
    frames_here, tokens, width = queries.shape
    group = lax.axis_index("tm")
    member = lax.axis_index("frame")
    x, y, z = member // (ROWS_Y * RING), (member // RING) % ROWS_Y, member % RING
    group_frames = frames_here * lax.axis_size("frame")
    listed = jnp.arange(key_frames.shape[0], dtype=jnp.int32)
    pick = lambda entry: jnp.sum(jnp.where(listed == entry, key_frames, 0))
    local = pick(group * KPG + x) - group * group_frames
    owner, slot = local // frames_here, local % frames_here
    owner_y, owner_z = (owner // RING) % ROWS_Y, owner % RING
    away = (z - owner_z) % RING

    share = tokens // QUARTERS

    def quarter(index):
        start = (index % QUARTERS) * share
        return jnp.concatenate(
            [lax.dynamic_slice(a, (slot, start, 0), (1, share, width)) for a in (keys, values)]
        )

    mine = quarter(z)
    second, right, left = send(quarter(z + 2), z=2), send(quarter(z + 1), z=1), send(quarter(z - 1), z=-1)
    mine = jnp.where(away == 1, right, jnp.where(away == RING - 1, left, jnp.where(away == 2, second, mine)))
    own_query = lax.dynamic_index_in_dim(queries, slot, 0, keepdims=True)
    order = jnp.stack([group ^ 1, group ^ 3, group, group ^ 2])
    frames_of = jnp.sum(jnp.where(listed == order[:, None] * KPG + x, key_frames, 0), axis=1)
    wanted = (frames_of // frames_here == order * lax.axis_size("frame") + member).astype(jnp.int32)
    facts = jnp.concatenate([wanted, slot[None]])
    own_query, facts, mine = lax.optimization_barrier((own_query, facts, mine))
    side_query = jnp.concatenate([own_query, swap_groups(own_query, 2)])
    filled = (away <= 2) | (away == RING - 1)
    mine = jnp.where(filled, mine, send(mine, z=RING // 2))
    mine = jnp.where(y == owner_y, mine, send(mine, y=1))
    side_query, mine = lax.optimization_barrier((side_query, mine))
    core_query = swap_groups(side_query, 1)
    second, right, left = send(mine, z=2), send(mine, z=1), send(mine, z=-1)
    half_a, half_b = jnp.stack([mine, right]), jnp.stack([left, second])
    right_a, left_b = send(half_a, x=1), send(half_b, x=-1)
    right_b, left_a = send(half_b, x=1), send(half_a, x=-1)
    far_a, far_b = send(right_a, x=1), send(left_b, x=-1)
    blocks = (half_a, half_b, right_a, right_b, left_a, left_b, far_a, far_b)

    kept, sent = joint_attend(facts, side_query, core_query, blocks)
    there = swap_groups(sent, 1)
    kept, sent = merge(facts, kept, there)
    there = swap_groups(sent, 2)
    plain = plain_attend(facts, queries, keys, values, blocks)
    return place(facts, kept, there, plain)


def solution(mesh):
    placed = P(("tm", "frame"), None, None)
    return jax.shard_map(
        body, mesh=mesh, in_specs=(placed, placed, placed, P()), out_specs=placed, check_vma=False
    )
```

```python
import jax
import jax.numpy as jnp
from jax import lax
from jax.experimental import pallas as pl
from jax.experimental.pallas import tpu as pltpu
from jax.sharding import PartitionSpec as P

HEADS = 20
HEAD_DIM = 64
KPG = 4
WIDE = 2 * HEAD_DIM
PAIRS = HEADS // 2
PLANES, ROWS_Y, RING = 4, 2, 8
QUARTERS = 4
VMEM_BYTES = 32 * 1024 * 1024
PLAIN_VMEM_BYTES = 60 * 1024 * 1024


def hop(x=0, y=0, z=0):
    pairs = []
    for member in range(PLANES * ROWS_Y * RING):
        px, py, pz = member // (ROWS_Y * RING), (member // RING) % ROWS_Y, member % RING
        target = ((px + x) % PLANES) * ROWS_Y * RING + ((py + y) % ROWS_Y) * RING + (pz + z) % RING
        pairs.append((member, target))
    return pairs


def send(array, **steps):
    return lax.ppermute(array, "frame", hop(**steps))


def swap_groups(array, mask):
    return lax.ppermute(array, "tm", [(group, group ^ mask) for group in range(4)])


def dot_last(a, b):
    return lax.dot_general(a, b, (((1,), (1,)), ((), ())), preferred_element_type=jnp.float32)


def dot_first(a, b):
    return lax.dot_general(a, b, (((0,), (0,)), ((), ())), preferred_element_type=jnp.float32)


def keep_one_head(array, other):
    low = lax.broadcasted_iota(jnp.int32, (1, WIDE), 1) < HEAD_DIM
    other = jnp.full((), other, array.dtype)
    return jnp.where(low, array, other), jnp.where(low, other, array)


def attend_pair(query, keys, values):
    sums, tops = [], []
    query = query * jnp.bfloat16(HEAD_DIM ** -0.5)
    for masked, extended in zip(keep_one_head(query, 0), keep_one_head(values, 1)):
        scores = dot_last(keys, masked)
        tops.append(jnp.max(scores, axis=0, keepdims=True))
        weights = jnp.exp(scores - tops[-1]).astype(jnp.bfloat16)
        sums.append(dot_first(extended, weights))
    totals = [sums[0][HEAD_DIM:HEAD_DIM + 1], sums[1][:1]]
    blended = jnp.concatenate([sums[0][:HEAD_DIM] / totals[0], sums[1][HEAD_DIM:] / totals[1]], axis=0)
    return blended.T, tops, totals


def columns_of(pair):
    return slice(pair * WIDE, (pair + 1) * WIDE)


def gathered(refs, which, columns):
    return [ref[:, which, :, columns].reshape(-1, WIDE) for ref in refs]


def whole(array):
    return pl.BlockSpec(array.shape, lambda i, *_: (0,) * array.ndim)


def plain_kernel(facts_ref, q_ref, k_ref, v_ref, *rest):
    group_refs, o_ref = rest[:-1], rest[-1]

    @pl.when((facts_ref[2] == 0) | (facts_ref[4] != pl.program_id(0)))
    def _():
        for pair in range(PAIRS):
            columns = columns_of(pair)
            keys = jnp.concatenate(gathered(group_refs, 0, columns) + [k_ref[0, :, columns]], axis=0)
            values = jnp.concatenate(gathered(group_refs, 1, columns) + [v_ref[0, :, columns]], axis=0)
            blended, _, _ = attend_pair(q_ref[0, :, columns], keys, values)
            o_ref[0, :, columns] = blended.astype(o_ref.dtype)


def plain_attend(facts, queries, keys, values, blocks):
    frames, tokens, width = queries.shape
    own = pl.BlockSpec((1, tokens, width), lambda i, f: (i, 0, 0))
    return pl.pallas_call(
        plain_kernel,
        grid_spec=pltpu.PrefetchScalarGridSpec(
            num_scalar_prefetch=1,
            grid=(frames,),
            in_specs=[own, own, own] + [whole(b) for b in blocks],
            out_specs=own,
        ),
        out_shape=jax.ShapeDtypeStruct(queries.shape, queries.dtype),
        compiler_params=pltpu.CompilerParams(vmem_limit_bytes=PLAIN_VMEM_BYTES),
        cost_estimate=pl.CostEstimate(
            flops=4 * frames * tokens * 640 * width,
            bytes_accessed=8 * frames * tokens * width + 4 * 512 * width,
            transcendentals=frames * tokens * 640 * HEADS,
        ),
        name="plain_attend",
    )(facts, queries, keys, values, *blocks)


def level_columns(levels):
    high = levels.astype(jnp.bfloat16).astype(jnp.float32)
    middle = (levels - high).astype(jnp.bfloat16).astype(jnp.float32)
    low = levels - high - middle
    return jnp.concatenate([high, middle, low, jnp.zeros_like(low)], axis=0).T.astype(jnp.bfloat16)


def levels_of(columns):
    parts = columns.astype(jnp.float32)
    return parts + pltpu.roll(parts, WIDE - 32, 1) + pltpu.roll(parts, WIDE - 64, 1)


def joint_kernel(facts_ref, side_ref, core_ref, *rest):
    group_refs, kept_ref, sent_ref, level_ref = rest[:-3], rest[-3], rest[-2], rest[-1]

    def attend(slot, q_ref, o_ref):
        level_ref[...] = jnp.zeros_like(level_ref)
        for pair in range(PAIRS):
            columns = columns_of(pair)
            keys = jnp.concatenate(gathered(group_refs, 0, columns), axis=0)
            values = jnp.concatenate(gathered(group_refs, 1, columns), axis=0)
            blended, tops, totals = attend_pair(q_ref[slot, :, columns], keys, values)
            o_ref[slot, :, columns] = blended.astype(o_ref.dtype)
            for head in range(2):
                level_ref[2 * pair + head:2 * pair + head + 1] = tops[head] + jnp.log(totals[head])
        o_ref[slot, :, HEADS * HEAD_DIM:] = level_columns(level_ref[...])

    for slot in range(2):
        pl.when(facts_ref[slot] != 0)(lambda: attend(slot, core_ref, sent_ref))
        pl.when(facts_ref[2 + slot] != 0)(lambda: attend(slot, side_ref, kept_ref))


SCALARS = pl.BlockSpec(memory_space=pltpu.SMEM)
VECTORS = pl.BlockSpec(memory_space=pltpu.VMEM)


def joint_attend(facts, side, core, blocks):
    frames, tokens, width = side.shape
    part = jax.ShapeDtypeStruct((frames, tokens, width + WIDE), jnp.bfloat16)
    return pl.pallas_call(
        joint_kernel,
        in_specs=[SCALARS] + [VECTORS] * (2 + len(blocks)),
        out_specs=[VECTORS, VECTORS],
        scratch_shapes=[pltpu.VMEM((32, tokens), jnp.float32)],
        out_shape=[part, part],
        compiler_params=pltpu.CompilerParams(vmem_limit_bytes=VMEM_BYTES),
        cost_estimate=pl.CostEstimate(
            flops=4 * tokens * 512 * width, bytes_accessed=4 * 512 * width, transcendentals=tokens * 512 * HEADS
        ),
        name="joint_attend",
    )(facts, side, core, *blocks)


def merged(a, b):
    width = HEADS * HEAD_DIM
    low = lax.broadcasted_iota(jnp.int32, (1, WIDE), 1) < HEAD_DIM
    level_a, level_b = levels_of(a[:, width:]), levels_of(b[:, width:])
    top = jnp.maximum(level_a, level_b)
    weight_a, weight_b = jnp.exp(level_a - top), jnp.exp(level_b - top)
    total = weight_a + weight_b
    weight_a, weight_b = weight_a / total, weight_b / total
    blended = []
    for pair in range(PAIRS):
        columns = columns_of(pair)
        first, second = slice(2 * pair, 2 * pair + 1), slice(2 * pair + 1, 2 * pair + 2)
        ratio_a = jnp.where(low, weight_a[:, first], weight_a[:, second])
        ratio_b = jnp.where(low, weight_b[:, first], weight_b[:, second])
        blended.append(a[:, columns].astype(jnp.float32) * ratio_a + b[:, columns].astype(jnp.float32) * ratio_b)
    return blended, top + jnp.log(total)


def merge_kernel(facts_ref, a_ref, b_ref, kept_ref, sent_ref):
    for slot, o_ref in enumerate((kept_ref, sent_ref)):

        @pl.when(facts_ref[2 + slot] != 0)
        def _():
            blended, level = merged(a_ref[slot], b_ref[slot])
            for pair in range(PAIRS):
                o_ref[:, columns_of(pair)] = blended[pair].astype(o_ref.dtype)
            o_ref[:, HEADS * HEAD_DIM:] = level_columns(level.T[:32])


def merge(facts, a, b):
    _, tokens, width = b.shape
    part = jax.ShapeDtypeStruct((tokens, width), b.dtype)
    return pl.pallas_call(
        merge_kernel,
        in_specs=[SCALARS, VECTORS, VECTORS],
        out_specs=[VECTORS, VECTORS],
        out_shape=[part, part],
        compiler_params=pltpu.CompilerParams(vmem_limit_bytes=VMEM_BYTES),
        name="merge_partials",
    )(facts, a, b)


def place_kernel(facts_ref, a_ref, b_ref, plain_ref, o_ref, rows_ref, done):
    @pl.when(facts_ref[2] != 0)
    def _():
        blended, _ = merged(a_ref[...], b_ref[...])
        for pair in range(PAIRS):
            rows_ref[0, :, columns_of(pair)] = blended[pair].astype(rows_ref.dtype)
        copy = pltpu.make_async_copy(rows_ref, o_ref.at[pl.ds(facts_ref[4], 1)], done)
        copy.start()
        copy.wait()


def place(facts, a, b, plain):
    return pl.pallas_call(
        place_kernel,
        in_specs=[SCALARS, VECTORS, VECTORS, pl.BlockSpec(memory_space=pl.ANY)],
        out_specs=pl.BlockSpec(memory_space=pl.ANY),
        scratch_shapes=[pltpu.VMEM((1, *plain.shape[1:]), plain.dtype), pltpu.SemaphoreType.DMA],
        out_shape=jax.ShapeDtypeStruct(plain.shape, plain.dtype),
        input_output_aliases={3: 0},
        compiler_params=pltpu.CompilerParams(vmem_limit_bytes=VMEM_BYTES),
        name="place_joint",
    )(facts, a, b, plain)


def quarters_kernel(frames_ref, keys_ref, values_ref, *rest):
    outputs, done = rest[:-1], rest[-1]
    group, member = lax.axis_index("tm"), lax.axis_index("frame")
    x, z = member // (ROWS_Y * RING), member % RING
    slot = frames_ref[group * KPG + x] % keys_ref.shape[0]
    copies = []
    for number, step in enumerate((0, 2, 1, QUARTERS - 1)):
        share = outputs[number].shape[1]
        start = pl.multiple_of((z + step) % QUARTERS * share, share)
        for which, source in enumerate((keys_ref, values_ref)):
            copies.append(
                pltpu.make_async_copy(
                    source.at[slot, pl.ds(start, share)], outputs[number].at[which], done.at[2 * number + which]
                )
            )
    for copy in copies:
        copy.start()
    for copy in copies:
        copy.wait()


def quarters(key_frames, keys, values):
    _, tokens, width = keys.shape
    anywhere = pl.BlockSpec(memory_space=pl.ANY)
    return pl.pallas_call(
        quarters_kernel,
        in_specs=[SCALARS, anywhere, anywhere],
        out_specs=[VECTORS] * 4,
        out_shape=[jax.ShapeDtypeStruct((2, tokens // QUARTERS, width), keys.dtype)] * 4,
        scratch_shapes=[pltpu.SemaphoreType.DMA((8,))],
        compiler_params=pltpu.CompilerParams(vmem_limit_bytes=PLAIN_VMEM_BYTES),
        name="quarters",
    )(key_frames, keys, values)


def body(queries, keys, values, key_frames):
    frames_here, tokens, width = queries.shape
    group = lax.axis_index("tm")
    member = lax.axis_index("frame")
    x, y, z = member // (ROWS_Y * RING), (member // RING) % ROWS_Y, member % RING
    group_frames = frames_here * lax.axis_size("frame")
    listed = jnp.arange(key_frames.shape[0], dtype=jnp.int32)
    pick = lambda entry: jnp.sum(jnp.where(listed == entry, key_frames, 0))
    local = pick(group * KPG + x) - group * group_frames
    owner, slot = local // frames_here, local % frames_here
    owner_y, owner_z = (owner // RING) % ROWS_Y, owner % RING
    away = (z - owner_z) % RING

    mine, for_second, for_right, for_left = quarters(key_frames, keys, values)
    second, right, left = send(for_second, z=2), send(for_right, z=1), send(for_left, z=-1)
    mine = jnp.where(away == 1, right, jnp.where(away == RING - 1, left, jnp.where(away == 2, second, mine)))
    own_query = lax.dynamic_index_in_dim(queries, slot, 0, keepdims=True)
    order = jnp.stack([group ^ 1, group ^ 3, group, group ^ 2])
    frames_of = jnp.sum(jnp.where(listed == order[:, None] * KPG + x, key_frames, 0), axis=1)
    wanted = (frames_of // frames_here == order * lax.axis_size("frame") + member).astype(jnp.int32)
    facts = jnp.concatenate([wanted, slot[None]])
    own_query, facts, mine = lax.optimization_barrier((own_query, facts, mine))
    side_query = jnp.concatenate([own_query, swap_groups(own_query, 2)])
    filled = (away <= 2) | (away == RING - 1)
    mine = jnp.where(filled, mine, send(mine, z=RING // 2))
    mine = jnp.where(y == owner_y, mine, send(mine, y=1))
    side_query, mine = lax.optimization_barrier((side_query, mine))
    core_query = swap_groups(side_query, 1)
    right, left, second = send(mine, z=1), send(mine, z=-1), send(mine, z=2)
    half_a, half_b = jnp.stack([mine, right]), jnp.stack([left, second])
    right_a, left_b = send(half_a, x=1), send(half_b, x=-1)
    right_b, left_a = send(half_b, x=1), send(half_a, x=-1)
    far_a, far_b = send(right_a, x=1), send(left_b, x=-1)
    blocks = (half_a, half_b, right_a, right_b, left_a, left_b, far_a, far_b)

    kept, sent = joint_attend(facts, side_query, core_query, blocks)
    there = swap_groups(sent, 1)
    kept, sent = merge(facts, kept, there)
    there = swap_groups(sent, 2)
    plain = plain_attend(facts, queries, keys, values, blocks)
    return place(facts, kept, there, plain)


def solution(mesh):
    placed = P(("tm", "frame"), None, None)
    return jax.shard_map(
        body, mesh=mesh, in_specs=(placed, placed, placed, P()), out_specs=placed, check_vma=False
    )
```
